128 devices in a mesh: spec: 16 (over y_lo, x, core), wave: 8 (over z, y_hi).
Axes of the slice: x: 4, y: 4 (y_hi: 2, y_lo: 2; y = y_hi * 2 + y_lo), z: 4, core: 2. Of those that a mesh axis runs over, the one named last changes fastest.
Arguments:
- spectra: bfloat16 [16384, 7168], P('spec', 'wave'), may hold values from 0.049804688 to 5
- offsets: int32 [64], P('spec'), may hold values from 0 to 7167, as said below
- cover_lo: int32 [16384], P('spec'), may hold values from 0 to 7167, as said below
- cover_hi: int32 [16384], P('spec'), may hold values from 5377 to 7168
- coefficients: float32 [16384, 128], P('spec'), may hold values from 0.03 to 0.3
- templates: float32 [128, 7168], P(None, 'wave'), may hold values from 0.03 to 0.3
Outputs:
- templates_new: float32 [128, 7168], P(None, 'wave')
- coefficients_new: float32 [16384, 128], P('spec')
The draws below stay inside these ranges and needn't reach their ends.
Inputs may be any that keep to these rules, and one draw needn't show every extreme that they name: `offsets`: the first block of each index of spec has an offset of at least 6272; the last block's offset is 7167. cover_lo < cover_hi for every spectrum; about one spectrum in eight has weight one only on its last 1 to 4 observed pixels, cover_hi = 7168; the others have cover_lo < 1792 and cover_hi > 5376.
All inputs are finite; a program needn't handle non-finite values.
Results may differ from the reference program's by a relative error of at most 0.0012.
Values may be sent and summed in bfloat16 or wider, within the bound.
No kernel may reach another device: no remote copies, remote signals or barrier semaphores. Data moves between devices by JAX's collectives and lax.ppermute only.
A program may use at most 128 MiB of HBM per device.

```python
import math
import jax
import jax.numpy as jnp
from jax import lax

PIX = 7168
RANK = 128
BLOCK = 256
SPEC_DEV = 1024
ITERS = 4
SPECTRA = 16384
BLOCKS = 64
N_SPEC = 16
N_WAVE = 8


def cover_pair(key):
    subkeys = jax.random.split(jax.random.fold_in(key, 7301), 4)
    wide_lo = jax.random.randint(subkeys[0], (SPECTRA,), 0, PIX // 4, dtype=jnp.int32)
    wide_hi = jax.random.randint(subkeys[1], (SPECTRA,), PIX - PIX // 4 + 1, PIX + 1, dtype=jnp.int32)
    narrow_len = jax.random.randint(subkeys[2], (SPECTRA,), 1, 5, dtype=jnp.int32)
    chosen = jax.random.randint(subkeys[3], (SPECTRA,), 0, 8, dtype=jnp.int32) == 0
    lower = jnp.where(chosen, PIX - narrow_len, wide_lo)
    upper = jnp.where(chosen, jnp.full((SPECTRA,), PIX, jnp.int32), wide_hi)
    return (lower, upper)


def draw_cover_lo(key, part):
    return cover_pair(key)[0]


def draw_cover_hi(key, part):
    return cover_pair(key)[1]


def draw_offsets(key, part):
    subkeys = jax.random.split(jax.random.fold_in(key, 5501), 2)
    spread = jax.random.randint(subkeys[0], (BLOCKS,), 0, PIX, dtype=jnp.int32)
    high = jax.random.randint(subkeys[1], (BLOCKS,), PIX - PIX // N_WAVE, PIX - PIX // (2 * N_WAVE), dtype=jnp.int32)
    index = jnp.arange(BLOCKS, dtype=jnp.int32)
    per_device = SPEC_DEV // BLOCK
    values = jnp.where(index % per_device == 0, high, spread)
    return jnp.where(index == BLOCKS - 1, jnp.full((BLOCKS,), PIX - 1, jnp.int32), values)


def steps_of(stream_key, dims, pieces, least, high):
    level, own = 1.0, jax.random.fold_in(stream_key, 6)
    for axis_at, parts in pieces:
        heights = jnp.exp(jax.random.uniform(jax.random.fold_in(own, axis_at), (parts,), jnp.float32, least / len(pieces), high / len(pieces)))
        level = level * jnp.repeat(heights, dims[axis_at] // parts).reshape([-1 if axis == axis_at else 1 for axis in range(len(dims))])
    return level


def setup_inputs(seed: int = 0) -> dict:
    keys = jax.random.split(jax.random.key(seed), 7)
    return {
        "spectra": jnp.clip(jnp.exp(math.log(5.0) - 4.609084 * jax.random.uniform(keys[0], (SPECTRA, PIX), jnp.float32) ** steps_of(keys[0], (SPECTRA, PIX), ((0, 16), (1, 8)), -0.2, 0.2)), 0.049804688, 5.0).astype(jnp.bfloat16),
        "offsets": draw_offsets(jax.random.fold_in(keys[6], 71), 0),
        "cover_lo": draw_cover_lo(jax.random.fold_in(keys[6], 71), 0),
        "cover_hi": draw_cover_hi(jax.random.fold_in(keys[6], 71), 0),
        "coefficients": jnp.clip(jnp.exp(math.log(0.3) - 2.3025852 * jax.random.uniform(keys[4], (SPECTRA, RANK), jnp.float32) ** steps_of(keys[4], (SPECTRA, RANK), ((0, 16),), -0.2, 0.2)), 0.03, 0.3),
        "templates": jnp.clip(jnp.exp(math.log(0.3) - 2.3025852 * jax.random.uniform(keys[5], (RANK, PIX), jnp.float32) ** steps_of(keys[5], (RANK, PIX), ((1, 8),), -0.2, 0.2)), 0.03, 0.3),
    }


def to_bf(value):
    return lax.optimization_barrier(value.astype(jnp.bfloat16)).astype(jnp.float32)


def matmul(left, right):
    return jnp.dot(left, right, precision=lax.Precision.HIGHEST)


def rest_span(fluxes, row_off, lo_rows, hi_rows):
    padded = jnp.concatenate([fluxes, jnp.zeros_like(fluxes)], axis=1)
    shifted = jax.vmap(lambda line, start: lax.dynamic_slice_in_dim(line, start, PIX, 0))(padded, row_off)
    pixel = jnp.arange(PIX, dtype=jnp.int32)
    observed = pixel[None, :] + row_off[:, None]
    inside = (observed >= lo_rows[:, None]) & (observed < hi_rows[:, None])
    return shifted.astype(jnp.float32), inside.astype(jnp.float32)


def ratio_of(rest, weight, model):
    return to_bf(jnp.where(weight > 0, rest / jnp.where(weight > 0, model, 1.0), 0.0))


def reference(spectra, offsets, cover_lo, cover_hi, coefficients, templates):
    row_off = jnp.repeat(offsets.astype(jnp.int32), BLOCK)
    flux_groups = spectra.reshape(N_SPEC, SPEC_DEV, PIX)
    off_groups = row_off.reshape(N_SPEC, SPEC_DEV)
    lo_groups = cover_lo.astype(jnp.int32).reshape(N_SPEC, SPEC_DEV)
    hi_groups = cover_hi.astype(jnp.int32).reshape(N_SPEC, SPEC_DEV)
    coef_groups = coefficients.reshape(N_SPEC, SPEC_DEV, RANK)
    temps = templates
    for update in range(ITERS):
        temps_bf = to_bf(temps)

        def stats(carry, item):
            fluxes, row_o, lo_rows, hi_rows, coef = item
            rest, weight = rest_span(fluxes, row_o, lo_rows, hi_rows)
            coef_bf = to_bf(coef)
            ratio = ratio_of(rest, weight, matmul(coef_bf, temps_bf))
            return (carry[0] + matmul(coef_bf.T, ratio), carry[1] + matmul(coef_bf.T, weight)), None

        start = jnp.zeros((RANK, PIX), jnp.float32)
        (num_t, den_t), unused = lax.scan(stats, (start, start), (flux_groups, off_groups, lo_groups, hi_groups, coef_groups))
        temps = temps * num_t / jnp.maximum(den_t, 1.0)
        temps_bf = to_bf(temps)

        def refresh(item):
            fluxes, row_o, lo_rows, hi_rows, coef = item
            rest, weight = rest_span(fluxes, row_o, lo_rows, hi_rows)
            coef_bf = to_bf(coef)
            ratio = ratio_of(rest, weight, matmul(coef_bf, temps_bf))
            num_c = matmul(ratio, temps_bf.T)
            den_c = matmul(weight, temps_bf.T)
            return coef * num_c / jnp.maximum(den_c, 1.0)

        coef_groups = lax.map(refresh, (flux_groups, off_groups, lo_groups, hi_groups, coef_groups))
    return temps, coef_groups.reshape(SPECTRA, RANK)
```

```python
import functools

import jax
import jax.numpy as jnp
from jax import lax
from jax.experimental import pallas as pl
from jax.experimental.pallas import tpu as pltpu
from jax.sharding import Mesh, PartitionSpec as P

ITERS = 4
PIX = 7168
RANK = 128
ROWS = 128
BOTH = 2 * ROWS
N_WAVE = 8
WIDTH = PIX // N_WAVE
CHIPS = 64
RUN = 56
MINE = CHIPS * RUN
STEP = 448
CODES = 32000.0
TINY = 1e-37

AXES = ("ylo", "x", "core", "zh", "zl", "yhi")
SPEC = ("ylo", "x", "core")
WAVE = ("zh", "zl", "yhi")
CHIP = ("zh", "zl", "yhi", "ylo", "x")

PARAMS = pltpu.CompilerParams(vmem_limit_bytes=56 * 1024 * 1024)
VM = pl.BlockSpec(memory_space=pltpu.VMEM)
SM = pl.BlockSpec(memory_space=pltpu.SMEM)


def shift_kernel(off_ref, obs_ref, lo_ref, hi_ref, out_ref, held):
    for w in range(N_WAVE):
        held[pl.ds(w * WIDTH, WIDTH), :] = obs_ref[w, pl.ds(0, WIDTH), :]
    held[pl.ds(PIX, 128), :] = jnp.zeros((128, ROWS), jnp.bfloat16)
    off = off_ref[0]
    fine = lax.rem(off, 16)
    coarse = off - fine
    lo = lo_ref[...]
    hi = hi_ref[...]
    row = lax.broadcasted_iota(jnp.int32, (2 * RUN, ROWS), 0)
    back = lax.rem(128 - fine, 128)

    def step(m, carry):
        first = 2 * RUN * m
        at = pl.multiple_of(jnp.minimum(first + coarse, PIX), 16)
        piece = held[pl.ds(at, 128), :].astype(jnp.float32)
        piece = pltpu.roll(piece, back, 0)[: 2 * RUN]
        seen = row + (first + off)
        inside = (seen >= lo) & (seen < hi)
        piece = jnp.where(inside, piece, 0.0)
        out_ref[0, m] = piece[:RUN].astype(jnp.bfloat16)
        out_ref[1, m] = piece[RUN:].astype(jnp.bfloat16)
        return carry

    lax.fori_loop(0, CHIPS, step, 0)


def ratio_of(own_ref, oth_ref, wt, hb, rows):
    model = jnp.dot(wt, hb, preferred_element_type=jnp.float32)
    rest = jnp.concatenate([own_ref[rows, :], oth_ref[rows, :]], axis=1).astype(jnp.float32)
    model = jnp.maximum(model, TINY)
    inv = pl.reciprocal(model, approx=True)
    inv = inv * (2.0 - model * inv)
    ratio = (rest * inv).astype(jnp.bfloat16)
    weight = jnp.where(rest > 0, 1.0, 0.0).astype(jnp.bfloat16)
    return ratio, weight


def swapped(x):
    return jnp.concatenate([x[:, ROWS:], x[:, :ROWS]], axis=1)


def template_kernel(first, *refs):
    if first:
        own_ref, oth_ref, wt_ref, ht_ref, out_ref, num_s, den_s = refs
        ht = ht_ref[...]
    else:
        own_ref, oth_ref, wt_ref, ht_ref, nd_ref, nd_oth_ref, out_ref, ht_out_ref, num_s, den_s = refs
        num = nd_ref[0] + swapped(nd_oth_ref[0])
        den = nd_ref[1] + swapped(nd_oth_ref[1])
        ht = ht_ref[...] * num / jnp.maximum(den, 1.0)
        ht_out_ref[...] = ht
    hb = ht.astype(jnp.bfloat16)

    def chunk(k, carry):
        top_n, top_d = carry
        rows = pl.ds(pl.multiple_of(k * STEP, STEP), STEP)
        ratio, weight = ratio_of(own_ref, oth_ref, wt_ref[rows, :], hb, rows)
        dims = (((1,), (1,)), ((), ()))
        num = lax.dot_general(ratio, hb, dims, preferred_element_type=jnp.float32)
        den = lax.dot_general(weight, hb, dims, preferred_element_type=jnp.float32)
        num_s[rows, :] = num
        den_s[rows, :] = den
        top_n = jnp.maximum(top_n, jnp.max(num.reshape(STEP // 8, 8, RANK), axis=0))
        top_d = jnp.maximum(top_d, jnp.max(den.reshape(STEP // 8, 8, RANK), axis=0))
        return top_n, top_d

    zero = jnp.zeros((8, RANK), jnp.float32)
    top_n, top_d = lax.fori_loop(0, MINE // STEP, chunk, (zero, zero))

    def power(top):
        top = jnp.max(top, axis=0, keepdims=True)
        power = jnp.ceil(jnp.log(jnp.maximum(top, 1e-30)) * 1.4426950408889634)
        return jnp.broadcast_to(power, (8, RANK))

    pow_n, pow_d = power(top_n), power(top_d)
    tail = jnp.concatenate([pow_n, pow_d], axis=0).astype(jnp.int32).astype(jnp.int16)
    scale_n = jnp.exp2(-pow_n) * CODES
    scale_d = jnp.exp2(-pow_d) * CODES

    def code(m, carry):
        rows = pl.ds(pl.multiple_of(m * RUN, 8), RUN)
        num = num_s[rows, :].reshape(RUN // 8, 8, RANK) * scale_n[None] + 0.5
        den = den_s[rows, :].reshape(RUN // 8, 8, RANK) * scale_d[None] + 0.5
        both = jnp.concatenate([num.reshape(RUN, RANK), den.reshape(RUN, RANK)], axis=0)
        out_ref[m, pl.ds(0, 2 * RUN), :] = both.astype(jnp.int32).astype(jnp.int16)
        out_ref[m, pl.ds(2 * RUN, 16), :] = tail
        return carry

    lax.fori_loop(0, CHIPS, code, 0, unroll=4)


def update_kernel(got_ref, w_ref, w_out_ref, send_ref):
    def add(j, carry):
        num, den = carry
        power = got_ref[j, pl.ds(2 * RUN, 16), :].astype(jnp.int32).astype(jnp.float32)
        scale = jnp.exp2(power) * (1.0 / CODES)
        both = got_ref[j, pl.ds(0, 2 * RUN), :].astype(jnp.int32).astype(jnp.float32)
        num = num + both[:RUN].reshape(RUN // 8, 8, RANK) * scale[None, :8]
        den = den + both[RUN:].reshape(RUN // 8, 8, RANK) * scale[None, 8:]
        return num, den

    zero = jnp.zeros((RUN // 8, 8, RANK), jnp.float32)
    num, den = lax.fori_loop(0, CHIPS, add, (zero, zero), unroll=4)
    num = num.reshape(RUN, RANK)
    den = den.reshape(RUN, RANK)
    w = w_ref[...] * num / jnp.maximum(den, 1.0)
    w_out_ref[...] = w
    sent = w.astype(send_ref.dtype)
    for j in range(CHIPS):
        send_ref[j] = sent


def coef_kernel(own_ref, oth_ref, wt_ref, ht_ref, nd_ref):
    hb = ht_ref[...].astype(jnp.bfloat16)

    def chunk(k, carry):
        num, den = carry
        rows = pl.ds(pl.multiple_of(k * STEP, STEP), STEP)
        wt = wt_ref[rows, :].astype(jnp.bfloat16)
        ratio, weight = ratio_of(own_ref, oth_ref, wt, hb, rows)
        dims = (((0,), (0,)), ((), ()))
        num = num + lax.dot_general(wt, ratio, dims, preferred_element_type=jnp.float32)
        den = den + lax.dot_general(wt, weight, dims, preferred_element_type=jnp.float32)
        return num, den

    zero = jnp.zeros((RANK, BOTH), jnp.float32)
    num, den = lax.fori_loop(0, MINE // STEP, chunk, (zero, zero))
    nd_ref[0] = num
    nd_ref[1] = den


def call(kernel, n_in, outs, scratch=(), smem=0):
    shapes = [jax.ShapeDtypeStruct(s, d) for s, d in outs]
    return pl.pallas_call(
        kernel,
        out_shape=shapes,
        in_specs=[SM] * smem + [VM] * (n_in - smem),
        out_specs=[VM] * len(shapes),
        scratch_shapes=list(scratch),
        compiler_params=PARAMS,
    )


def to_partner(x):
    return lax.ppermute(x, "core", [(0, 1), (1, 0)])


def shards(spectra, offsets, cover_lo, cover_hi, coefficients, templates):
    bf = jnp.bfloat16
    f32 = jnp.float32
    core = lax.axis_index("core")
    wave = lax.axis_index(WAVE)
    spec = lax.axis_index(SPEC)

    temps_t = templates.T
    runs = temps_t.reshape(N_WAVE, 2, RUN, RANK)
    first_w = lax.dynamic_index_in_dim(runs, core, 1, keepdims=False).reshape(WIDTH // 2, RANK)
    flux_t = spectra.reshape(N_WAVE, ROWS, WIDTH).transpose(0, 2, 1)
    first_b = jnp.broadcast_to(first_w.astype(bf)[None], (N_WAVE, WIDTH // 2, RANK))
    got = lax.all_to_all(jnp.concatenate([flux_t, first_b], axis=1), WAVE, 0, 0, tiled=True)
    wt = got[:, WIDTH:].reshape(MINE, RANK)
    w_own = lax.dynamic_slice_in_dim(temps_t, spec * RUN, RUN, 0)

    start = wave * ROWS
    off = lax.dynamic_slice_in_dim(offsets, wave // 2, 1, 0)
    lo = lax.dynamic_slice_in_dim(cover_lo, start, ROWS, 0).reshape(1, ROWS)
    hi = lax.dynamic_slice_in_dim(cover_hi, start, ROWS, 0).reshape(1, ROWS)
    (rest,) = call(
        shift_kernel,
        4,
        [((2, CHIPS, RUN, ROWS), bf)],
        [pltpu.VMEM((PIX + 128, ROWS), bf)],
        smem=1,
    )(off, got, lo, hi)
    rest = rest.reshape(2, MINE, ROWS)
    own = lax.dynamic_index_in_dim(rest, core, 0, keepdims=False)
    oth = to_partner(lax.dynamic_index_in_dim(rest, 1 - core, 0, keepdims=False))

    h_own = lax.dynamic_slice_in_dim(coefficients, start, ROWS, 0).T
    ht = jnp.concatenate([h_own, to_partner(h_own)], axis=1)

    codes = ((CHIPS, 2 * RUN + 16, RANK), jnp.int16)
    nd_shape = ((2, RANK, BOTH), f32)
    stats = [pltpu.VMEM((MINE, RANK), f32)] * 2
    for update in range(ITERS):
        if update == 0:
            (sums,) = call(functools.partial(template_kernel, True), 4, [codes], stats)(own, oth, wt, ht)
        else:
            sums, ht = call(
                functools.partial(template_kernel, False), 6, [codes, ((RANK, BOTH), f32)], stats
            )(own, oth, wt, ht, nd, nd_oth)
        got_sums = lax.all_to_all(sums, CHIP, 0, 0, tiled=True)
        sent = f32 if update == ITERS - 1 else bf
        w_own, send = call(
            update_kernel, 2, [((RUN, RANK), f32), ((CHIPS, RUN, RANK), sent)]
        )(got_sums, w_own)
        wt = lax.all_to_all(send, CHIP, 0, 0, tiled=True).reshape(MINE, RANK)
        (nd,) = call(coef_kernel, 4, [nd_shape])(own, oth, wt, ht)
        if update < ITERS - 1:
            nd_oth = to_partner(nd)

    mine = lax.dynamic_slice_in_dim(wt, wave * (WIDTH // 2), WIDTH // 2, 0)
    theirs = to_partner(mine)
    even = jnp.where(core == 0, mine, theirs).reshape(N_WAVE, 1, RUN, RANK)
    odd = jnp.where(core == 0, theirs, mine).reshape(N_WAVE, 1, RUN, RANK)
    temps = jnp.concatenate([even, odd], axis=1).reshape(WIDTH, RANK).T

    nd_half = nd[:, :, :ROWS] + to_partner(nd[:, :, ROWS:])
    h_new = (ht[:, :ROWS] * nd_half[0] / jnp.maximum(nd_half[1], 1.0)).T
    coef = lax.all_to_all(
        jnp.broadcast_to(h_new[None], (N_WAVE, ROWS, RANK)), WAVE, 0, 0, tiled=True
    ).reshape(N_WAVE * ROWS, RANK)
    return (temps, coef)


def solution(mesh):
    fine = Mesh(mesh.devices.reshape(2, 4, 2, 2, 2, 2), AXES)
    in_specs = (
        P(SPEC, WAVE),
        P(SPEC),
        P(SPEC),
        P(SPEC),
        P(SPEC, None),
        P(None, WAVE),
    )
    out_specs = (P(None, WAVE), P(SPEC, None))
    return jax.shard_map(shards, mesh=fine, in_specs=in_specs, out_specs=out_specs, check_vma=False)
```

```python
import functools

import jax
import jax.numpy as jnp
from jax import lax
from jax.experimental import pallas as pl
from jax.experimental.pallas import tpu as pltpu
from jax.sharding import Mesh, PartitionSpec as P

ITERS = 4
PIX = 7168
RANK = 128
ROWS = 128
PAIR = 2 * ROWS
HELD = 4 * ROWS
N_WAVE = 8
WIDTH = PIX // N_WAVE
CHIPS = 32
RUN = 56
MINE = CHIPS * RUN
STEP = 448
TINY = 1e-37
LEVELS = 64000.0
MIDDLE = 32000.0
TAIL = 8
LOG2E = 1.4426950408889634

AXES = ("ylo", "x", "core", "zh", "zl", "yhi")
SPEC = ("ylo", "x", "core")
WAVE = ("zh", "zl", "yhi")
CHIP = ("zh", "zl", "ylo", "x")
FIRST = (((0,), (0,)), ((), ()))
LAST = (((1,), (1,)), ((), ()))

PARAMS = pltpu.CompilerParams(vmem_limit_bytes=16 * 1024 * 1024)
VM = pl.BlockSpec(memory_space=pltpu.VMEM)
SM = pl.BlockSpec(memory_space=pltpu.SMEM)


def to_int(x):
    return x.astype(jnp.int32)


def scale_of(top):
    return jnp.ceil(jnp.log(jnp.maximum(top, 1e-30)) * (64 * LOG2E))


def codes_of(x, power):
    return to_int(x * (jnp.exp2(power * (-1 / 64)) * LEVELS) + 0.5) - int(MIDDLE)


def unit_of(power):
    return jnp.exp2(power * (1 / 64)) * (1 / LEVELS)


def tail_of(pow_a, pow_b):
    cols = pow_a.shape[1]
    half = (TAIL // 2, cols)
    return to_int(
        jnp.concatenate([jnp.broadcast_to(pow_a, half), jnp.broadcast_to(pow_b, half)], axis=0)
    )


def coded(num, den):
    pow_n = scale_of(jnp.max(num, axis=0, keepdims=True))
    pow_d = scale_of(jnp.max(den, axis=0, keepdims=True))
    return jnp.concatenate(
        [codes_of(num, pow_n), codes_of(den, pow_d), tail_of(pow_n, pow_d)], axis=0
    ).astype(jnp.int16)


def decoded(codes):
    x = codes.astype(jnp.int32).astype(jnp.float32)
    rows = (x.shape[0] - TAIL) // 2
    unit_n = unit_of(x[2 * rows : 2 * rows + 1])
    unit_d = unit_of(x[2 * rows + TAIL // 2 : 2 * rows + TAIL // 2 + 1])
    return (x[:rows] + MIDDLE) * unit_n, (x[rows : 2 * rows] + MIDDLE) * unit_d


def coded_one(x):
    power = scale_of(jnp.max(x, axis=0, keepdims=True))
    return jnp.concatenate([codes_of(x, power), tail_of(power, power)], axis=0).astype(jnp.int16)


def decoded_one(codes):
    x = codes.astype(jnp.int32).astype(jnp.float32)
    rows = x.shape[0] - TAIL
    return (x[:rows] + MIDDLE) * unit_of(x[rows : rows + 1])


def shift_kernel(leave, sc_ref, obs_ref, lo_ref, hi_ref, a_ref, b_ref, held):
    for w in range(N_WAVE):
        held[pl.ds(w * WIDTH, WIDTH), :] = obs_ref[w]
    held[pl.ds(PIX, 128), :] = jnp.zeros((128, ROWS), jnp.bfloat16)
    off, core, side = sc_ref[0], sc_ref[1], sc_ref[2]
    if leave:
        side = 1 - side
    lo = lo_ref[...]
    hi = hi_ref[...]
    row = lax.broadcasted_iota(jnp.int32, (RUN, ROWS), 0)

    def step(k, carry):
        for out_ref, set_core in ((a_ref, core), (b_ref, 1 - core)):
            at = 2 * RUN * (k + 8 * (k // 8) + 8 * side) + RUN * set_core + off
            fine = lax.rem(at, 16)
            start = pl.multiple_of(jnp.minimum(at - fine, PIX), 16)
            piece = held[pl.ds(start, 80), :].astype(jnp.float32)
            piece = pltpu.roll(piece, lax.rem(80 - fine, 80), 0)[:RUN]
            seen = row + at
            piece = jnp.where((seen >= lo) & (seen < hi), piece, 0.0)
            out_ref[k] = piece.astype(jnp.bfloat16)
        return carry

    lax.fori_loop(0, CHIPS, step, 0, unroll=2)


def ratio_of(rest_refs, wt, hb, rows):
    model = jnp.dot(wt, hb, preferred_element_type=jnp.float32)
    rest = jnp.concatenate([ref[rows, :] for ref in rest_refs], axis=1).astype(jnp.float32)
    inv = pl.reciprocal(jnp.maximum(model, TINY), approx=True)
    ratio = (rest * inv).astype(jnp.bfloat16)
    weight = jnp.where(rest > 0, 1.0, 0.0).astype(jnp.bfloat16)
    return ratio, weight


def swapped(x):
    return jnp.concatenate([x[:, ROWS:], x[:, :ROWS]], axis=1)


def template_kernel(r0, r1, r2, r3, wt_ref, hb_ref, hb_oth_ref, out_ref, num_s, den_s):
    hb = jnp.concatenate([hb_ref[...], hb_oth_ref[...]], axis=1)

    def chunk(k, carry):
        top_n, top_d = carry
        rows = pl.ds(pl.multiple_of(k * STEP, STEP), STEP)
        ratio, weight = ratio_of((r0, r1, r2, r3), wt_ref[rows, :], hb, rows)
        num = lax.dot_general(ratio, hb, LAST, preferred_element_type=jnp.float32)
        den = lax.dot_general(weight, hb, LAST, preferred_element_type=jnp.float32)
        num_s[rows, :] = num
        den_s[rows, :] = den
        top_n = jnp.maximum(top_n, jnp.max(num.reshape(STEP // 8, 8, RANK), axis=0))
        top_d = jnp.maximum(top_d, jnp.max(den.reshape(STEP // 8, 8, RANK), axis=0))
        return top_n, top_d

    zero = jnp.zeros((8, RANK), jnp.float32)
    top_n, top_d = lax.fori_loop(0, MINE // STEP, chunk, (zero, zero))
    pow_n = scale_of(jnp.max(top_n, axis=0, keepdims=True))
    pow_d = scale_of(jnp.max(top_d, axis=0, keepdims=True))
    tail = tail_of(pow_n, pow_d)

    def code(m, carry):
        rows = pl.ds(pl.multiple_of(m * RUN, 8), RUN)
        num = codes_of(num_s[rows, :], pow_n)
        den = codes_of(den_s[rows, :], pow_d)
        out_ref[m] = jnp.concatenate([num, den, tail], axis=0).astype(jnp.int16)
        return carry

    lax.fori_loop(0, CHIPS, code, 0, unroll=4)


def update_kernel(last, got_ref, w_ref, w_out_ref, send_ref):
    def add(j, carry):
        num, den = decoded(got_ref[j])
        return carry[0] + num, carry[1] + den

    zero = jnp.zeros((RUN, RANK), jnp.float32)
    num, den = lax.fori_loop(0, CHIPS, add, (zero, zero), unroll=4)
    w = w_ref[...] * num / jnp.maximum(den, 1.0)
    w_out_ref[...] = w
    sent = coded_one(w) if last else w.astype(jnp.bfloat16)
    for j in range(CHIPS):
        send_ref[j] = sent


def unpack_kernel(codes_ref, wt_ref):
    def step(j, carry):
        wt_ref[j] = decoded_one(codes_ref[j]).astype(jnp.bfloat16)
        return carry

    lax.fori_loop(0, CHIPS, step, 0, unroll=4)


def coef_kernel(r0, r1, r2, r3, wt_ref, hb_ref, hb_oth_ref, keep_ref, give_ref):
    hb = jnp.concatenate([hb_ref[...], hb_oth_ref[...]], axis=1)

    def chunk(k, carry):
        num, den = carry
        rows = pl.ds(pl.multiple_of(k * STEP, STEP), STEP)
        wt = wt_ref[rows, :]
        ratio, weight = ratio_of((r0, r1, r2, r3), wt, hb, rows)
        num = num + lax.dot_general(wt, ratio, FIRST, preferred_element_type=jnp.float32)
        den = den + lax.dot_general(wt, weight, FIRST, preferred_element_type=jnp.float32)
        return num, den

    zero = jnp.zeros((RANK, HELD), jnp.float32)
    num, den = lax.fori_loop(0, MINE // STEP, chunk, (zero, zero))
    keep_ref[0] = num[:, :PAIR]
    keep_ref[1] = den[:, :PAIR]
    give_ref[0] = num[:, PAIR:]
    give_ref[1] = den[:, PAIR:]


def fold_kernel(a_ref, b_ref, out_ref):
    out_ref[...] = coded(a_ref[0] + b_ref[0], a_ref[1] + b_ref[1])


def fold_last_kernel(a_ref, b_ref, keep_ref, out_ref):
    num = a_ref[0] + b_ref[0]
    den = a_ref[1] + b_ref[1]
    keep_ref[0] = num[:, :ROWS]
    keep_ref[1] = den[:, :ROWS]
    out_ref[...] = coded(num[:, ROWS:], den[:, ROWS:])


def step_kernel(mine_ref, oth_ref, h_ref, h_out_ref, hb_out_ref):
    num, den = decoded(mine_ref[...])
    num_o, den_o = decoded(oth_ref[...])
    ht = h_ref[...] * (num + swapped(num_o)) / jnp.maximum(den + swapped(den_o), 1.0)
    h_out_ref[...] = ht
    hb_out_ref[...] = ht.astype(jnp.bfloat16)


def step_last_kernel(mine_ref, oth_ref, h_ref, out_ref):
    num, den = decoded(oth_ref[...])
    ht = h_ref[:, pl.ds(0, ROWS)] * (mine_ref[0] + num) / jnp.maximum(mine_ref[1] + den, 1.0)
    sent = coded_one(ht)
    for j in range(N_WAVE):
        out_ref[j] = sent


def coef_out_kernel(got_ref, out_ref):
    for j in range(N_WAVE):
        out_ref[pl.ds(j * ROWS, ROWS), :] = decoded_one(got_ref[j]).T


def temps_out_kernel(core_ref, mine_ref, theirs_ref, out_ref):
    swap = core_ref[0] == 1
    pieces = []
    for j in range(N_WAVE):
        mine = decoded_one(mine_ref[j])
        theirs = decoded_one(theirs_ref[j])
        pieces += [jnp.where(swap, theirs, mine), jnp.where(swap, mine, theirs)]
    whole = jnp.concatenate(pieces, axis=0)
    for j in range(WIDTH // 128):
        out_ref[:, pl.ds(j * 128, 128)] = whole[j * 128 : (j + 1) * 128].T


def call(kernel, n_in, outs, scratch=(), smem=0):
    shapes = [jax.ShapeDtypeStruct(s, d) for s, d in outs]
    return pl.pallas_call(
        kernel,
        out_shape=shapes,
        in_specs=[SM] * smem + [VM] * (n_in - smem),
        out_specs=[VM] * len(shapes),
        scratch_shapes=list(scratch),
        compiler_params=PARAMS,
    )


def over(axis, x):
    return lax.ppermute(x, axis, [(0, 1), (1, 0)])


def shards(spectra, offsets, cover_lo, cover_hi, coefficients, templates):
    bf = jnp.bfloat16
    f32 = jnp.float32
    i16 = jnp.int16
    core = lax.axis_index("core")
    side = lax.axis_index("yhi")
    wave = lax.axis_index(WAVE)
    spec = lax.axis_index(SPEC)

    flux_t = spectra.reshape(N_WAVE, ROWS, WIDTH).transpose(0, 2, 1)
    got = lax.all_to_all(flux_t, WAVE, 0, 0, tiled=True)

    start = wave * ROWS
    off = lax.dynamic_slice_in_dim(offsets, wave // 2, 1, 0)
    scalars = jnp.concatenate([off, core[None], side[None]])
    lo = lax.dynamic_slice_in_dim(cover_lo, start, ROWS, 0).reshape(1, ROWS)
    hi = lax.dynamic_slice_in_dim(cover_hi, start, ROWS, 0).reshape(1, ROWS)
    run = ((CHIPS, RUN, ROWS), bf)
    held = [pltpu.VMEM((PIX + 128, ROWS), bf)]
    leave, leave_core = call(functools.partial(shift_kernel, True), 4, [run] * 2, held, smem=1)(
        scalars, got, lo, hi
    )
    r1 = over("yhi", leave)
    r3 = over("yhi", over("core", leave_core))
    r0, stay_core = call(functools.partial(shift_kernel, False), 4, [run] * 2, held, smem=1)(
        scalars, got, lo, hi
    )
    r2 = over("core", stay_core)
    rest = [r.reshape(MINE, ROWS) for r in (r0, r1, r2, r3)]

    temps_t = templates.T
    runs = temps_t.reshape(N_WAVE, 2, RUN, RANK)
    first_w = lax.dynamic_index_in_dim(runs, core, 1, keepdims=False).reshape(WIDTH // 2, RANK)
    first_b = jnp.broadcast_to(first_w.astype(bf)[None], (4, WIDTH // 2, RANK))
    first_b, _ = lax.optimization_barrier((first_b, r0))
    wt = lax.all_to_all(first_b, ("zh", "zl"), 0, 0, tiled=True).reshape(MINE, RANK)
    w_own = lax.dynamic_slice_in_dim(temps_t, spec * RUN, RUN, 0)

    h_own = lax.dynamic_slice_in_dim(coefficients, start, ROWS, 0)
    h_oth = lax.dynamic_slice_in_dim(coefficients, (wave ^ 1) * ROWS, ROWS, 0)
    ht = jnp.concatenate([h_own, h_oth], axis=0).T
    hb = ht.astype(bf)

    sums_shape = ((CHIPS, 2 * RUN + TAIL, RANK), i16)
    nd_shape = ((2, RANK, PAIR), f32)
    stats = [pltpu.VMEM((MINE, RANK), f32)] * 2
    for update in range(ITERS):
        last = update == ITERS - 1
        hb_oth = over("core", hb)
        (sums,) = call(template_kernel, 7, [sums_shape], stats)(*rest, wt, hb, hb_oth)
        got_sums = lax.all_to_all(sums, CHIP, 0, 0, tiled=True)
        send_shape = ((CHIPS, RUN + TAIL, RANK), i16) if last else ((CHIPS, RUN, RANK), bf)
        w_own, send = call(
            functools.partial(update_kernel, last), 2, [((RUN, RANK), f32), send_shape]
        )(got_sums, w_own)
        wt = lax.all_to_all(send, CHIP, 0, 0, tiled=True)
        if last:
            w_codes = wt
            (wt,) = call(unpack_kernel, 1, [((CHIPS, RUN, RANK), bf)])(wt)
        wt = wt.reshape(MINE, RANK)
        keep, give = call(coef_kernel, 7, [nd_shape] * 2)(*rest, wt, hb, hb_oth)
        got_nd = over("core", give)
        if not last:
            (nd,) = call(fold_kernel, 2, [((2 * RANK + TAIL, PAIR), i16)])(keep, got_nd)
            ht, hb = call(step_kernel, 3, [((RANK, PAIR), f32), ((RANK, PAIR), bf)])(
                nd, over("yhi", nd), ht
            )

    nd, nd_give = call(
        fold_last_kernel, 2, [((2, RANK, ROWS), f32), ((2 * RANK + TAIL, ROWS), i16)]
    )(keep, got_nd)
    (h_send,) = call(step_last_kernel, 3, [((N_WAVE, RANK + TAIL, ROWS), i16)])(
        nd, over("yhi", nd_give), ht
    )
    h_got = lax.all_to_all(h_send, WAVE, 0, 0, tiled=True)
    (coef,) = call(coef_out_kernel, 1, [((N_WAVE * ROWS, RANK), f32)])(h_got)

    mine = lax.dynamic_slice_in_dim(w_codes, (wave // 2) * N_WAVE, N_WAVE, 0)
    (temps,) = call(temps_out_kernel, 3, [((RANK, WIDTH), f32)], smem=1)(
        core[None], mine, over("core", mine)
    )
    return (temps, coef)


def solution(mesh):
    fine = Mesh(mesh.devices.reshape(2, 4, 2, 2, 2, 2), AXES)
    in_specs = (
        P(SPEC, WAVE),
        P(SPEC),
        P(SPEC),
        P(SPEC),
        P(SPEC, None),
        P(None, WAVE),
    )
    out_specs = (P(None, WAVE), P(SPEC, None))
    return jax.shard_map(shards, mesh=fine, in_specs=in_specs, out_specs=out_specs, check_vma=False)
```
